32 devices in a mesh: grp: 4 (over x, core), dom: 8 (over z, y).
Axes of the slice: x: 2, y: 2, z: 4, core: 2. Of those that a mesh axis runs over, the one named last changes fastest.
Arguments:
- tracers: float32 [2, 80, 262144], P(None, None, ('grp', 'dom')), may hold values from -6 to 6
- mix_weights: float32 [6, 262144], P(None, ('grp', 'dom')), may hold values from 0 to 0.16
- neighbors: int32 [6, 262144], P(None, ('grp', 'dom')), may hold values from 0 to 10239
- send_list: int32 [65536], P(('grp', 'dom')), may hold values from 0 to 8191
- slot_cell: int32 [65536], P(('grp', 'dom')), may hold values from 0 to 8191
- slot_owner: int32 [65536, 1], P(('grp', 'dom')), may hold values from 0 to 31; in each aligned block of 2048 rows (0 to 2047, 2048 to 4095, ...) at most 128 rows name the same one
- slot_node: int32 [65536], P(('grp', 'dom')), may hold values from 0 to 4095
- thickness: float32 [128, 1024], P('dom', 'grp'), may hold values from 0.6 to 1.9
- friction: float32 [128, 1024], P('dom', 'grp'), may hold values from 0.2 to 2
- driving: float32 [128, 1024], P('dom', 'grp'), may hold values from -6 to 6
- velocity: float32 [128, 1024], P('dom', 'grp'), may hold values from -4 to 4
Outputs:
- ocean_state: float32 [2, 80, 262144], P(None, None, ('grp', 'dom'))
- ice_thickness: float32 [128, 1024], P('dom', 'grp')
- ice_velocity: float32 [128, 1024], P('dom', 'grp')
The draws below stay inside these ranges and needn't reach their ends.
Inputs may be any that keep to these rules, and one draw needn't show every extreme that they name: `slot_owner`: among the 2048 slots of one block at most 128 name the same owner, a bound that some block reaches.
All inputs are finite; a program needn't handle non-finite values.
Results may differ from the reference program's by a relative error of at most 0.0033.
Values sent between devices are 32-bit elements; how exact they have to be, the bound alone decides.
A program may use at most 192 MiB of HBM per device.

```python
import math
import jax
import jax.numpy as jnp
import numpy as np

LEV = 80
NBR = 6
CELLS = 8192
HS = 1024
MS = 2048
CAP = 128
IR = 16
IC = 256
ITERS = 4
N_GRP = 4
N_DOM = 8
DEVICES = 32


def place_ends(drawn, key, smallest, high):
    place = [jax.random.randint(jax.random.fold_in(key, axis), (), 0, length) for axis, length in enumerate(drawn.shape)]
    main_axis = drawn.shape.index(max(drawn.shape))
    beside = place[:main_axis] + [(place[main_axis] + 1) % drawn.shape[main_axis]] + place[main_axis + 1:]
    return drawn.at[tuple(place)].set(smallest).at[tuple(beside)].set(high)


def level_of(key, shape, split, smallest, high):
    gain = 1.0
    for dim, parts in split:
        steps = jax.random.uniform(jax.random.fold_in(jax.random.fold_in(key, 6), dim), (parts,), jnp.float32, smallest / len(split), high / len(split))
        gain = gain * jnp.repeat(jnp.exp(steps), shape[dim] // parts).reshape((-1,) + (1,) * (len(shape) - 1 - dim))
    return gain


def shared_out(own_key, own, number, rows, number_of, top, limit, lean):
    order = jax.random.permutation(own_key, number_of)
    packed, usual = load_shares(number_of, rows * top, limit, lean, True), load_shares(number_of, rows * top, limit, lean, False)
    places = jnp.arange(number_of)

    def named(tallies, offset_by):
        used = int((tallies > 0).sum())
        fixed = max(1, used // 4)
        shifted = fixed + (places - fixed + offset_by * (used - fixed)) % max(1, number_of - fixed)
        return jnp.zeros((number_of,), jnp.int32).at[order[jnp.where(places < fixed, places, shifted)]].set(jnp.asarray(tallies, jnp.int32))

    tallies = jnp.where(number % 4 == 0, named(packed, number // 4), named(usual, number - number // 4 - 1))
    mixed = jax.random.permutation(jax.random.fold_in(own, 3), number_of)
    source_of, receiver = mixed[0:number_of // 2 * 2:2], mixed[1:number_of // 2 * 2:2]
    room = jnp.minimum(tallies[source_of] - 1, limit - tallies[receiver]) // 2
    room = jnp.where((source_of == order[0]) | (receiver == order[0]) | (tallies[receiver] == 0), 0, jnp.maximum(room, 0))
    shifted = jax.random.randint(jax.random.fold_in(own, 4), (number_of // 2,), 0, 1 << 20) % (room + 1)
    tallies = tallies.at[source_of].add(-shifted).at[receiver].add(shifted)
    items = jnp.searchsorted(jnp.cumsum(tallies), jnp.arange(rows * top), side="right").astype(jnp.int32)
    table = items.reshape(top, rows).T
    table = table[jax.random.permutation(jax.random.fold_in(own, 1), rows)]
    offset_by = jax.random.randint(jax.random.fold_in(own, 2), (rows, 1), 0, top)
    return jnp.take_along_axis(table, (jnp.arange(top)[None, :] + offset_by) % top, axis=1)


def load_shares(number_of, total, reach, lean, full):
    weights = [(1 << 20) // math.isqrt(standing ** lean) + 1 for standing in range(1, number_of + 1)]
    largest = reach if full else min(reach, max(-(-total // number_of), total * weights[0] // sum(weights)))
    least = 1 if total - largest >= number_of - 1 else 0
    holding, surplus = [largest] + [least] * (number_of - 1), total - largest - least * (number_of - 1)
    while surplus > 0:
        free = [i for i in range(1, number_of) if holding[i] < largest] or [i for i in range(1, number_of) if holding[i] < reach]
        pool, left = sum([weights[i] for i in free]), surplus
        for i in free:
            extra = min(reach - holding[i], max(1, left * weights[i] // pool), surplus)
            holding[i] = holding[i] + extra
            surplus = surplus - extra
    return np.array(holding)


def scatter_about(key, shape, scale, most, split=(), held_as=jnp.bfloat16):
    result = jax.random.normal(key, shape, jnp.float32) * scale
    if len(split) > 0:
        result = level_of(key, shape, split, -0.22, 0.18) * result
    return jnp.clip(result, min=-most, max=most).astype(held_as)


def setup_inputs(seed: int = 0) -> dict:
    seeds = jax.random.split(jax.random.key(seed), 12)
    tracers = scatter_about(seeds[0], (2, LEV, CELLS * DEVICES), 1.0, 6.0, ((2, 32),), jnp.float32)
    mix_weights = jnp.clip(0.16 * jax.random.uniform(seeds[1], (NBR, CELLS * DEVICES), jnp.float32) ** level_of(seeds[1], (NBR, CELLS * DEVICES), ((1, 32),), -0.2, 0.2), 0.0, 0.16)
    neighbors = place_ends(jax.random.randint(seeds[2], (NBR, CELLS * DEVICES), 0, CELLS + 2 * HS), jax.random.fold_in(seeds[2], 1), 0, (CELLS + 2 * HS) - 1).astype(jnp.int32)
    send_list = place_ends(jax.random.randint(seeds[3], (2 * HS * DEVICES,), 0, CELLS), jax.random.fold_in(seeds[3], 1), 0, CELLS - 1).astype(jnp.int32)
    slot_cell = place_ends(jax.random.randint(seeds[4], (MS * DEVICES,), 0, CELLS), jax.random.fold_in(seeds[4], 1), 0, CELLS - 1).astype(jnp.int32)
    slot_owner_keys = jax.random.split(jax.random.fold_in(seeds[5], 1), (MS * DEVICES) // MS)
    slot_owner_turns = jax.random.permutation(jax.random.fold_in(seeds[5], 3), (MS * DEVICES) // MS)
    slot_owner = jax.vmap(lambda own, number: shared_out(jax.random.fold_in(seeds[5], 2), own, number, MS, DEVICES, 1, CAP, 2))(slot_owner_keys, slot_owner_turns).reshape((MS * DEVICES, 1))
    slot_node = place_ends(jax.random.randint(seeds[6], (MS * DEVICES,), 0, IR * IC), jax.random.fold_in(seeds[6], 1), 0, (IR * IC) - 1).astype(jnp.int32)
    thickness = jnp.clip(0.6 + 1.3 * jax.random.uniform(seeds[7], (IR * N_DOM, IC * N_GRP), jnp.float32) ** level_of(seeds[7], (IR * N_DOM, IC * N_GRP), ((0, 8), (1, 4)), -0.2, 0.2), 0.6, 1.9)
    friction = jnp.clip(jnp.exp(math.log(2.0) - 2.3025851 * jax.random.uniform(seeds[8], (IR * N_DOM, IC * N_GRP), jnp.float32) ** level_of(seeds[8], (IR * N_DOM, IC * N_GRP), ((0, 8), (1, 4)), -0.2, 0.2)), 0.2, 2.0)
    driving = scatter_about(seeds[9], (IR * N_DOM, IC * N_GRP), 1.0, 6.0, ((0, 8), (1, 4)), jnp.float32)
    velocity = scatter_about(seeds[10], (IR * N_DOM, IC * N_GRP), 0.5, 4.0, ((0, 8), (1, 4)), jnp.float32)
    return dict(tracers=tracers, mix_weights=mix_weights, neighbors=neighbors, send_list=send_list, slot_cell=slot_cell, slot_owner=slot_owner, slot_node=slot_node, thickness=thickness, friction=friction, driving=driving, velocity=velocity)


VERT_MIX = 0.2
COLUMN_DEPTH = 2.0
SPREAD_INV = 3.0
DRAFT_RATIO = 0.89
FREEZE_SALT = 0.0573
FREEZE_DEPTH = 0.76
THIN_RATE = 0.05
HEAT_SINK = 12.0
SALT_SINK = 6.0
VISC_FLOOR = 0.05


def vertical_mix(quantity):
    shifted_up = jnp.concatenate([quantity[:, :1], quantity[:, :-1]], axis=1)
    shifted_down = jnp.concatenate([quantity[:, 1:], quantity[:, -1:]], axis=1)
    return shifted_up + shifted_down - 2.0 * quantity


def level_share(depths, levels):
    centers = (jnp.arange(levels, dtype=jnp.float32) + 0.5) * (COLUMN_DEPTH / levels)
    kernel = jnp.exp(-SPREAD_INV * (centers[None, :] - depths[:, None]) ** 2)
    return kernel / jnp.sum(kernel, axis=1, keepdims=True)


def melt_from(heat_rows, salt_rows, depths):
    level_part = level_share(depths, heat_rows.shape[1])
    heat_mean = jnp.sum(level_part * heat_rows, axis=1)
    salt_mean = jnp.sum(level_part * salt_rows, axis=1)
    return heat_mean - FREEZE_SALT * salt_mean + FREEZE_DEPTH * depths, level_part


def ice_image(quantity, viscosity, friction, padded, padded_visc):
    northern = padded[2:, 1:-1]
    southern = padded[:-2, 1:-1]
    eastern = padded[1:-1, 2:]
    western = padded[1:-1, :-2]
    west_visc = padded_visc[1:-1, :-2]
    south_visc = padded_visc[:-2, 1:-1]
    image = friction * quantity + viscosity * (2.0 * quantity - eastern - northern)
    image = image + west_visc * (quantity - western) + south_visc * (quantity - southern)
    return image, west_visc, south_visc


def reference(tracers, mix_weights, neighbors, send_list, slot_cell, slot_owner, slot_node, thickness, friction, driving, velocity):
    devices = N_GRP * N_DOM
    blocks = tracers.reshape(2, LEV, N_GRP, N_DOM, CELLS)
    full_shape = (2, LEV, N_GRP, N_DOM, 2 * HS)
    sends = jnp.broadcast_to(send_list.reshape(1, 1, N_GRP, N_DOM, 2 * HS), full_shape)
    outgoing = jnp.take_along_axis(blocks, sends, axis=4)
    from_left = jnp.roll(outgoing[..., HS:], 1, axis=3)
    from_right = jnp.roll(outgoing[..., :HS], -1, axis=3)
    extended = jnp.concatenate([blocks, from_left, from_right], axis=4)
    links = neighbors.reshape(NBR, N_GRP, N_DOM, CELLS)
    coupling = mix_weights.reshape(NBR, N_GRP, N_DOM, CELLS)
    horizontal = jnp.zeros_like(blocks)
    for neighbor in range(NBR):
        pointer = jnp.broadcast_to(links[neighbor][None, None], blocks.shape)
        gathered = jnp.take_along_axis(extended, pointer, axis=4)
        horizontal = horizontal + coupling[neighbor] * (gathered - blocks)
    mixed_state = (blocks + horizontal + VERT_MIX * vertical_mix(blocks)).reshape(2, LEV, CELLS * devices)

    source = jnp.repeat(jnp.arange(devices, dtype=jnp.int32), MS)
    cell_ids = source * CELLS + slot_cell
    owners = slot_owner[:, 0]
    node_row = (owners % N_DOM) * IR + slot_node // IC
    node_col = (owners // N_DOM) * IC + slot_node % IC
    depths = DRAFT_RATIO * thickness[node_row, node_col]
    columns = mixed_state[:, :, cell_ids]
    melt_rate, level_part = melt_from(columns[0].T, columns[1].T, depths)
    weighted = melt_rate[:, None] * level_part
    sink_rates = jnp.array([HEAT_SINK, SALT_SINK], dtype=jnp.float32)
    increments = -sink_rates[:, None, None] * weighted.T[None]
    ocean_state = mixed_state.at[:, :, cell_ids].add(increments)
    ice_thick = thickness.at[node_row, node_col].add(-THIN_RATE * melt_rate)

    viscosity = VISC_FLOOR + 0.5 * ice_thick * ice_thick
    forcing = driving * ice_thick
    padded_visc = jnp.pad(viscosity, 1)

    def operate(quantity):
        return ice_image(quantity, viscosity, friction, jnp.pad(quantity, 1), padded_visc)

    image, west_visc, south_visc = operate(velocity)
    diagonal = friction + 2.0 * viscosity + west_visc + south_visc
    solution = velocity
    residual = forcing - image
    precond = residual / diagonal
    direction = precond
    norm_now = jnp.sum(residual * precond)
    for sweep in range(ITERS):
        image = operate(direction)[0]
        step_length = norm_now / jnp.sum(direction * image)
        solution = solution + step_length * direction
        residual = residual - step_length * image
        precond = residual / diagonal
        if sweep + 1 < ITERS:
            norm_next = jnp.sum(residual * precond)
            direction = precond + (norm_next / norm_now) * direction
            norm_now = norm_next
    return ocean_state, ice_thick, solution
```

```python
import functools

import jax
import jax.numpy as jnp
from jax import lax
from jax.experimental import pallas as pl
from jax.experimental.pallas import tpu as pltpu
from jax.sharding import PartitionSpec as P

ITERS = 4
VERT_MIX = 0.2
COLUMN_DEPTH = 2.0
SPREAD_INV = 3.0
DRAFT_RATIO = 0.89
FREEZE_SALT = 0.0573
FREEZE_DEPTH = 0.76
THIN_RATE = 0.05
HEAT_SINK = 12.0
SALT_SINK = 6.0
VISC_FLOOR = 0.05
LANES = 128
MESH = pl.DeviceIdType.MESH
VMEM = pltpu.VMEM
SMEM = pltpu.SMEM
BIG = 58 * 1024 * 1024


def split(value):
    high = value.astype(jnp.bfloat16)
    return high, (value - high.astype(jnp.float32)).astype(jnp.bfloat16)


def turn_kernel(send_ref, tracers_ref, table_ref, picked_ref):
    levels, cells = tracers_ref.shape[1:]
    tile = 512

    @pl.loop(0, cells // tile)
    def _(step):
        at = pl.ds(pl.multiple_of(step * tile, tile), tile)
        for kind in range(2):
            block = tracers_ref[kind, :, at]
            block = jnp.concatenate(
                [block, jnp.zeros((LANES - levels, tile), jnp.float32)], axis=0
            )
            table_ref[kind, at, :] = block.T

    @pl.loop(0, send_ref.shape[0] // 16)
    def _(step):
        for inner in range(16):
            item = step * 16 + inner
            cell = send_ref[item]
            for kind in range(2):
                picked_ref[kind, pl.ds(item, 1), :] = table_ref[kind, pl.ds(cell, 1), :]


def mix_kernel(levels, nbr_ref, weight_ref, own_ref, table_ref, left_ref, right_ref,
               mixed_ref, extended, sem):
    step = pl.program_id(0)
    cells = table_ref.shape[1]
    rim = left_ref.shape[1]
    block = mixed_ref.shape[1]

    @pl.when(step == 0)
    def _():
        copies = [
            pltpu.make_async_copy(table_ref, extended.at[:, pl.ds(0, cells)], sem.at[0]),
            pltpu.make_async_copy(left_ref, extended.at[:, pl.ds(cells, rim)], sem.at[1]),
            pltpu.make_async_copy(right_ref, extended.at[:, pl.ds(cells + rim, rim)], sem.at[2]),
        ]
        for copy in copies:
            copy.start()
        for copy in copies:
            copy.wait()

    unroll = 8

    @pl.loop(0, block // unroll)
    def _(outer):
        base = outer * unroll
        for inner in range(unroll):
            cell = base + inner
            own = own_ref[0, cell]
            here = step * block + cell
            sums = [own * extended[kind, pl.ds(here, 1), :] for kind in range(2)]
            for k in range(nbr_ref.shape[0]):
                source = nbr_ref[k, cell]
                weight = weight_ref[k, cell]
                for kind in range(2):
                    sums[kind] = sums[kind] + weight * extended[kind, pl.ds(source, 1), :]
            for kind in range(2):
                mixed_ref[kind, pl.ds(cell, 1), :] = sums[kind]

    tile = 128
    lane = lax.broadcasted_iota(jnp.int32, (tile, LANES), 1)

    @pl.loop(0, block // tile)
    def _(part):
        first = pl.multiple_of(part * tile, tile)
        at = pl.ds(pl.multiple_of(step * block + first, tile), tile)
        for kind in range(2):
            column = extended[kind, at, :]
            above = jnp.where(lane == 0, column, pltpu.roll(column, 1, 1))
            below = jnp.where(lane == levels - 1, column, pltpu.roll(column, LANES - 1, 1))
            mixed_ref[kind, pl.ds(first, tile), :] += VERT_MIX * (above + below)


def melt_kernel(cell_ref, row_col_ref, row_lane_ref, col_ref, thick_ref, mixed_ref,
                ocean_ref, sums_ref, state, heat_cols, salt_cols, weighted, sem):
    levels, cells = ocean_ref.shape[1:]
    slots = heat_cols.shape[0]
    rows, width = thick_ref.shape
    copy = pltpu.make_async_copy(mixed_ref, state, sem)
    copy.start()
    copy.wait()

    @pl.loop(0, slots // 16)
    def _(step):
        for inner in range(16):
            slot = step * 16 + inner
            cell = cell_ref[slot]
            heat_cols[pl.ds(slot, 1), :] = state[0, pl.ds(cell, 1), :]
            salt_cols[pl.ds(slot, 1), :] = state[1, pl.ds(cell, 1), :]

    high, low = split(thick_ref[...])
    tile = 256
    sums_ref[...] = jnp.zeros_like(sums_ref)

    @pl.loop(0, slots // tile)
    def _(step):
        at = pl.ds(pl.multiple_of(step * tile, tile), tile)
        pick = (
            lax.broadcasted_iota(jnp.int32, (tile, rows), 1) == row_col_ref[at, :]
        ).astype(jnp.float32).astype(jnp.bfloat16)
        found = jnp.dot(pick, high, preferred_element_type=jnp.float32)
        found = found + jnp.dot(pick, low, preferred_element_type=jnp.float32)
        here = lax.broadcasted_iota(jnp.int32, (tile, width), 1) == col_ref[at, :]
        depth = DRAFT_RATIO * jnp.sum(jnp.where(here, found, 0.0), axis=1, keepdims=True)
        lane = lax.broadcasted_iota(jnp.int32, (tile, LANES), 1)
        center = (lane.astype(jnp.float32) + 0.5) * (COLUMN_DEPTH / levels)
        share = jnp.where(lane < levels, jnp.exp(-SPREAD_INV * (center - depth) ** 2), 0.0)
        share = share / jnp.sum(share, axis=1, keepdims=True)
        taken = share * (heat_cols[at, :] - FREEZE_SALT * salt_cols[at, :])
        melt = jnp.sum(taken, axis=1, keepdims=True) + FREEZE_DEPTH * depth
        weighted[at, :] = melt * share
        melt_high, melt_low = split(jnp.where(here, melt, 0.0))
        put = (
            lax.broadcasted_iota(jnp.int32, (rows, tile), 0) == row_lane_ref[:, at]
        ).astype(jnp.float32).astype(jnp.bfloat16)
        sums_ref[...] += jnp.dot(put, melt_high, preferred_element_type=jnp.float32) + jnp.dot(
            put, melt_low, preferred_element_type=jnp.float32
        )

    @pl.loop(0, slots // 16)
    def _(step):
        for inner in range(16):
            slot = step * 16 + inner
            cell = pl.ds(cell_ref[slot], 1)
            part = weighted[pl.ds(slot, 1), :]
            state[0, cell, :] = state[0, cell, :] - HEAT_SINK * part
            state[1, cell, :] = state[1, cell, :] - SALT_SINK * part

    span = 512

    @pl.loop(0, cells // span)
    def _(step):
        at = pl.ds(pl.multiple_of(step * span, span), span)
        for kind in range(2):
            ocean_ref[kind, :, at] = state[kind, at, :].T[:levels]


def ice_kernel(groups, domains, sums_ref, thick_ref, friction_ref, driving_ref, velocity_ref,
               ice_ref, out_ref, strip_in, strip, block_in, strips, diag, visc, iterate, resid, direct,
               send_a, recv_a, send_b, recv_b, send_c, recv_c, send_d, recv_d):
    g = lax.axis_index("grp")
    d = lax.axis_index("dom")
    rows, cols = thick_ref.shape
    tall = domains * rows
    height, width = friction_ref.shape

    barrier = pltpu.get_barrier_semaphore()
    for off in range(1, groups):
        pl.semaphore_signal(barrier, inc=1, device_id=((g + off) % groups, d), device_id_type=MESH)
    for off in range(1, domains):
        pl.semaphore_signal(barrier, inc=1, device_id=(g, (d + off) % domains), device_id_type=MESH)
    pl.semaphore_wait(barrier, groups + domains - 2)

    def strip_rows(which):
        return pl.ds(pl.multiple_of(which * tall, tall), tall)

    def block_rows(which):
        return pl.ds(pl.multiple_of(which * rows, rows), rows)

    def send(src, dst, sems, off, device):
        copy = pltpu.make_async_remote_copy(
            src_ref=src, dst_ref=dst, send_sem=sems[0].at[off - 1], recv_sem=sems[1].at[off - 1],
            device_id=device, device_id_type=MESH,
        )
        copy.start()
        return copy

    copies = []
    for off in range(1, groups):
        other = (g + off) % groups
        copies.append(send(sums_ref.at[strip_rows(other)], strip_in.at[off - 1],
                           (send_a, recv_a), off, (other, d)))
    total = sums_ref[strip_rows(g), :]
    for copy in copies:
        copy.wait()
    for off in range(1, groups):
        total = total + strip_in[off - 1]
    strip[...] = total

    copies = []
    for off in range(1, domains):
        other = (d + off) % domains
        copies.append(send(strip.at[block_rows(other)], block_in.at[off - 1],
                           (send_b, recv_b), off, (g, other)))
    melted = strip[block_rows(d), :]
    for copy in copies:
        copy.wait()
    for off in range(1, domains):
        melted = melted + block_in[off - 1]
    ice = thick_ref[...] - THIN_RATE * melted
    ice_ref[...] = ice
    strips[g, block_rows(d), :] = ice

    copies = []
    for off in range(1, domains):
        other = (d + off) % domains
        copies.append(send(strips.at[g, block_rows(d)], strips.at[g, block_rows(d)],
                           (send_c, recv_c), off, (g, other)))
    for copy in copies:
        copy.wait()
    copies = []
    for off in range(1, groups):
        other = (g + off) % groups
        copies.append(send(strips.at[g], strips.at[g], (send_d, recv_d), off, (other, d)))
    for copy in copies:
        copy.wait()

    thickness = jnp.concatenate([strips[i] for i in range(groups)], axis=1)
    row = lax.broadcasted_iota(jnp.int32, (height, width), 0)
    col = lax.broadcasted_iota(jnp.int32, (height, width), 1)

    def west(value):
        return jnp.where(col == 0, 0.0, pltpu.roll(value, 1, 1))

    def east(value):
        return jnp.where(col == width - 1, 0.0, pltpu.roll(value, width - 1, 1))

    def south(value):
        return jnp.where(row == 0, 0.0, pltpu.roll(value, 1, 0))

    def north(value):
        return jnp.where(row == height - 1, 0.0, pltpu.roll(value, height - 1, 0))

    visc[...] = VISC_FLOOR + 0.5 * thickness * thickness
    diag[...] = friction_ref[...] + 2.0 * visc[...] + west(visc[...]) + south(visc[...])

    def operate(value):
        viscosity = visc[...]
        image = friction_ref[...] * value + viscosity * (2.0 * value - east(value) - north(value))
        image = image + west(viscosity) * (value - west(value))
        return image + south(viscosity) * (value - south(value))

    iterate[...] = velocity_ref[...]
    resid[...] = driving_ref[...] * thickness - operate(velocity_ref[...])
    direct[...] = resid[...] / diag[...]
    norm = jnp.sum(resid[...] * direct[...], keepdims=True)

    def sweep(_, norm):
        direction = direct[...]
        image = operate(direction)
        length = norm / jnp.sum(direction * image, keepdims=True)
        iterate[...] += length * direction
        residual = resid[...] - length * image
        resid[...] = residual
        precond = residual / diag[...]
        following = jnp.sum(residual * precond, keepdims=True)
        direct[...] = precond + following / norm * direction
        return following

    lax.fori_loop(0, ITERS - 1, sweep, norm)
    direction = direct[...]
    image = operate(direction)
    last = jnp.sum(resid[...] * (resid[...] / diag[...]), keepdims=True)
    length = last / jnp.sum(direction * image, keepdims=True)
    iterate[...] += length * direction
    out_ref[...] = iterate[block_rows(d), pl.ds(pl.multiple_of(g * cols, cols), cols)]


def local(tracers, mix_weights, neighbors, send_list, slot_cell, slot_owner, slot_node,
          thickness, friction, driving, velocity):
    levels, cells = tracers.shape[1:]
    groups = lax.axis_size("grp")
    domains = lax.axis_size("dom")
    devices = groups * domains
    slots = slot_cell.shape[0]
    rim = send_list.shape[0] // 2
    rows, cols = thickness.shape
    f32 = jnp.float32
    whole = pl.BlockSpec(memory_space=VMEM)
    scalars = pl.BlockSpec(memory_space=SMEM)
    anywhere = pl.BlockSpec(memory_space=pl.ANY)
    big = pltpu.CompilerParams(vmem_limit_bytes=BIG)

    shards = lax.all_gather(
        jnp.concatenate([thickness, friction, driving, velocity], axis=0), ("grp", "dom"), axis=0
    ).reshape(devices, 4, rows, cols)
    thick_table = shards[:, 0].reshape(devices * rows, cols)
    grids = [
        shards[:, i].reshape(groups, domains * rows, cols).transpose(1, 0, 2).reshape(
            domains * rows, groups * cols)
        for i in range(1, 4)
    ]

    table, picked = pl.pallas_call(
        turn_kernel,
        out_shape=(jax.ShapeDtypeStruct((2, cells, LANES), f32),
                   jax.ShapeDtypeStruct((2, 2 * rim, LANES), f32)),
        in_specs=[scalars, whole],
        out_specs=(whole, whole),
        compiler_params=big,
    )(send_list, tracers)
    forward = [(i, (i + 1) % domains) for i in range(domains)]
    backward = [(target, source) for source, target in forward]
    left = lax.ppermute(picked[:, rim:], "dom", forward)
    right = lax.ppermute(picked[:, :rim], "dom", backward)

    own_weight = (1.0 - 2.0 * VERT_MIX) - jnp.sum(mix_weights, axis=0, keepdims=True)
    block = 1024
    count = neighbors.shape[0]
    mixed = pl.pallas_call(
        functools.partial(mix_kernel, levels),
        grid=(cells // block,),
        out_shape=jax.ShapeDtypeStruct((2, cells, LANES), f32),
        in_specs=[
            pl.BlockSpec((count, block), lambda i: (0, i), memory_space=SMEM),
            pl.BlockSpec((count, block), lambda i: (0, i), memory_space=SMEM),
            pl.BlockSpec((1, block), lambda i: (0, i), memory_space=SMEM),
            anywhere, anywhere, anywhere,
        ],
        out_specs=pl.BlockSpec((2, block, LANES), lambda i: (0, i, 0)),
        scratch_shapes=[pltpu.VMEM((2, cells + 2 * rim, LANES), f32), pltpu.SemaphoreType.DMA((3,))],
        compiler_params=big,
        cost_estimate=pl.CostEstimate(flops=200_000_000, bytes_accessed=200_000_000, transcendentals=0),
    )(neighbors, mix_weights, own_weight, table, left, right)

    grid_row = slot_owner[:, 0] * rows + slot_node // cols
    grid_col = slot_node % cols
    ocean, sums = pl.pallas_call(
        melt_kernel,
        out_shape=(jax.ShapeDtypeStruct((2, levels, cells), f32),
                   jax.ShapeDtypeStruct((devices * rows, cols), f32)),
        in_specs=[scalars, whole, whole, whole, whole, anywhere],
        out_specs=(whole, whole),
        scratch_shapes=[
            pltpu.VMEM((2, cells, LANES), f32),
            pltpu.VMEM((slots, LANES), f32),
            pltpu.VMEM((slots, LANES), f32),
            pltpu.VMEM((slots, LANES), f32),
            pltpu.SemaphoreType.DMA,
        ],
        compiler_params=big,
    )(slot_cell, grid_row[:, None], grid_row[None, :], grid_col[:, None], thick_table, mixed)

    grid_shape = (domains * rows, groups * cols)
    dma = pltpu.SemaphoreType.DMA
    ice, iterate = pl.pallas_call(
        functools.partial(ice_kernel, groups, domains),
        out_shape=(jax.ShapeDtypeStruct((rows, cols), f32),) * 2,
        in_specs=[whole] * 5,
        out_specs=(whole, whole),
        scratch_shapes=[
            pltpu.VMEM((groups - 1, domains * rows, cols), f32),
            pltpu.VMEM((domains * rows, cols), f32),
            pltpu.VMEM((domains - 1, rows, cols), f32),
            pltpu.VMEM((groups, domains * rows, cols), f32),
        ] + [pltpu.VMEM(grid_shape, f32)] * 5 + [
            dma((groups - 1,)), dma((groups - 1,)), dma((domains - 1,)), dma((domains - 1,)),
            dma((domains - 1,)), dma((domains - 1,)), dma((groups - 1,)), dma((groups - 1,)),
        ],
        compiler_params=pltpu.CompilerParams(
            collective_id=0, has_side_effects=True, vmem_limit_bytes=BIG
        ),
    )(sums, thickness, *grids)
    return ocean, ice, iterate


def solution(mesh):
    return jax.shard_map(
        local,
        mesh=mesh,
        in_specs=(
            P(None, None, ("grp", "dom")),
            P(None, ("grp", "dom")),
            P(None, ("grp", "dom")),
            P(("grp", "dom")),
            P(("grp", "dom")),
            P(("grp", "dom"), None),
            P(("grp", "dom")),
            P("dom", "grp"),
            P("dom", "grp"),
            P("dom", "grp"),
            P("dom", "grp"),
        ),
        out_specs=(P(None, None, ("grp", "dom")), P("dom", "grp"), P("dom", "grp")),
        check_vma=False,
    )
```

```python
import functools

import jax
import jax.numpy as jnp
from jax import lax
from jax.experimental import pallas as pl
from jax.experimental.pallas import tpu as pltpu
from jax.sharding import PartitionSpec as P

ITERS = 4
VERT_MIX = 0.2
COLUMN_DEPTH = 2.0
SPREAD_INV = 3.0
DRAFT_RATIO = 0.89
FREEZE_SALT = 0.0573
FREEZE_DEPTH = 0.76
THIN_RATE = 0.05
HEAT_SINK = 12.0
SALT_SINK = 6.0
VISC_FLOOR = 0.05
LANES = 128
MESH = pl.DeviceIdType.MESH
VMEM = pltpu.VMEM
SMEM = pltpu.SMEM
LEAD = 2
GROUP = 32
BIG = 58 * 1024 * 1024


def split(value):
    high = value.astype(jnp.bfloat16)
    return high, (value - high.astype(jnp.float32)).astype(jnp.bfloat16)


def columns_of(block):
    pad = jnp.zeros((LANES - block.shape[0], block.shape[1]), jnp.float32)
    return jnp.concatenate([block, pad], axis=0).T


def turn_kernel(send_ref, tracers_ref, table_ref, first_ref, second_ref, picked):
    levels, cells = tracers_ref.shape[1:]
    rim = first_ref.shape[2]
    tile = 512

    @pl.loop(0, cells // tile)
    def _(step):
        at = pl.ds(pl.multiple_of(step * tile, tile), tile)
        for kind in range(2):
            table_ref[kind, at, :] = columns_of(tracers_ref[kind, :, at])

    @pl.loop(0, send_ref.shape[0] // 32)
    def _(step):
        for inner in range(32):
            item = step * 32 + inner
            cell = send_ref[item]
            for kind in range(2):
                picked[kind, pl.ds(item, 1), :] = table_ref[kind, pl.ds(cell, 1), :]

    for half, out_ref in enumerate((first_ref, second_ref)):
        for start in range(0, rim, tile):
            for kind in range(2):
                rows = picked[kind, half * rim + start : half * rim + start + tile, :]
                out_ref[kind, :, start : start + tile] = rows.T[:levels]


def add_columns(nbr_ref, weight_ref, table, mixed_ref, first, unroll):
    for inner in range(unroll):
        cell = first + inner
        sums = [mixed_ref[kind, pl.ds(cell, 1), :] for kind in range(2)]
        for k in range(nbr_ref.shape[0]):
            source = nbr_ref[k, cell]
            weight = weight_ref[k, cell]
            for kind in range(2):
                sums[kind] = sums[kind] + weight * table[kind, pl.ds(source, 1), :]
        for kind in range(2):
            mixed_ref[kind, pl.ds(cell, 1), :] = sums[kind]


def near_kernel(nbr_ref, weight_ref, own_ref, tracers_ref, table_ref, mixed_ref, table, sem):
    block = mixed_ref.shape[1]

    @pl.when(pl.program_id(0) == 0)
    def _():
        copy = pltpu.make_async_copy(table_ref, table, sem)
        copy.start()
        copy.wait()

    tile = 512
    for start in range(0, block, tile):
        for kind in range(2):
            here = tracers_ref[kind, :, start : start + tile]
            above = jnp.concatenate([here[:1], here[:-1]], axis=0)
            below = jnp.concatenate([here[1:], here[-1:]], axis=0)
            value = own_ref[:, start : start + tile] * here + VERT_MIX * (above + below)
            mixed_ref[kind, start : start + tile, :] = columns_of(value)

    @pl.loop(0, block // GROUP)
    def _(outer):
        add_columns(nbr_ref, weight_ref, table, mixed_ref, outer * GROUP, GROUP)


def far_kernel(flag_ref, nbr_ref, weight_ref, lead_nbr_ref, lead_weight_ref, table_ref, left_ref, right_ref,
               near_ref, mixed_ref, extended, sem):
    step = pl.program_id(0)
    cells = table_ref.shape[1]
    rim = left_ref.shape[2]
    block = mixed_ref.shape[1]
    tile = 512

    @pl.when(step == 0)
    def _():
        copy = pltpu.make_async_copy(table_ref, extended.at[:, pl.ds(0, cells)], sem)
        copy.start()
        for side, ref in enumerate((left_ref, right_ref)):
            for start in range(0, rim, tile):
                for kind in range(2):
                    first = cells + side * rim + start
                    extended[kind, first : first + tile, :] = columns_of(ref[kind, :, start : start + tile])
        copy.wait()

    for kind in range(2):
        mixed_ref[kind] = near_ref[kind]

    @pl.loop(0, block // GROUP)
    def _(outer):
        first = outer * GROUP
        add_columns(nbr_ref, weight_ref, extended, mixed_ref, first, GROUP)

        @pl.when(flag_ref[step * (block // GROUP) + outer] > 0)
        def _():
            @pl.loop(0, GROUP)
            def _(inner):
                add_columns(lead_nbr_ref, lead_weight_ref, extended, mixed_ref, first + inner, 1)


def melt_kernel(cell_ref, row_col_ref, row_lane_ref, col_ref, thick_ref, mixed_ref,
                ocean_ref, sums_ref, state, heat_cols, salt_cols, weighted, sem):
    levels, cells = ocean_ref.shape[1:]
    slots = heat_cols.shape[0]
    rows, width = thick_ref.shape
    copy = pltpu.make_async_copy(mixed_ref, state, sem)
    copy.start()
    copy.wait()

    @pl.loop(0, slots // 32)
    def _(step):
        for inner in range(32):
            slot = step * 32 + inner
            cell = cell_ref[slot]
            heat_cols[pl.ds(slot, 1), :] = state[0, pl.ds(cell, 1), :]
            salt_cols[pl.ds(slot, 1), :] = state[1, pl.ds(cell, 1), :]

    high, low = split(thick_ref[...])
    tile = 256
    sums_ref[...] = jnp.zeros_like(sums_ref)

    @pl.loop(0, slots // tile)
    def _(step):
        at = pl.ds(pl.multiple_of(step * tile, tile), tile)
        pick = (
            lax.broadcasted_iota(jnp.int32, (tile, rows), 1) == row_col_ref[at, :]
        ).astype(jnp.float32).astype(jnp.bfloat16)
        found = jnp.dot(pick, high, preferred_element_type=jnp.float32)
        found = found + jnp.dot(pick, low, preferred_element_type=jnp.float32)
        here = lax.broadcasted_iota(jnp.int32, (tile, width), 1) == col_ref[at, :]
        depth = DRAFT_RATIO * jnp.sum(jnp.where(here, found, 0.0), axis=1, keepdims=True)
        lane = lax.broadcasted_iota(jnp.int32, (tile, LANES), 1)
        center = (lane.astype(jnp.float32) + 0.5) * (COLUMN_DEPTH / levels)
        share = jnp.where(lane < levels, jnp.exp(-SPREAD_INV * (center - depth) ** 2), 0.0)
        share = share / jnp.sum(share, axis=1, keepdims=True)
        taken = share * (heat_cols[at, :] - FREEZE_SALT * salt_cols[at, :])
        melt = jnp.sum(taken, axis=1, keepdims=True) + FREEZE_DEPTH * depth
        weighted[at, :] = melt * share
        melt_high, melt_low = split(jnp.where(here, melt, 0.0))
        put = (
            lax.broadcasted_iota(jnp.int32, (rows, tile), 0) == row_lane_ref[:, at]
        ).astype(jnp.float32).astype(jnp.bfloat16)
        sums_ref[...] += jnp.dot(put, melt_high, preferred_element_type=jnp.float32) + jnp.dot(
            put, melt_low, preferred_element_type=jnp.float32
        )

    @pl.loop(0, slots // 16)
    def _(step):
        for inner in range(16):
            slot = step * 16 + inner
            cell = pl.ds(cell_ref[slot], 1)
            part = weighted[pl.ds(slot, 1), :]
            heat = state[0, cell, :] - HEAT_SINK * part
            salt = state[1, cell, :] - SALT_SINK * part
            state[0, cell, :] = heat
            state[1, cell, :] = salt

    span = 512

    @pl.loop(0, cells // span)
    def _(step):
        at = pl.ds(pl.multiple_of(step * span, span), span)
        for kind in range(2):
            ocean_ref[kind, :, at] = state[kind, at, :].T[:levels]


def ice_kernel(groups, domains, sums_ref, thick_ref, friction_ref, driving_ref, velocity_ref,
               ice_ref, out_ref, strip_in, strip, block_in, strips, diag, visc, iterate, resid, direct,
               send_a, recv_a, send_b, recv_b, send_c, recv_c, send_d, recv_d):
    g = lax.axis_index("grp")
    d = lax.axis_index("dom")
    rows, cols = thick_ref.shape
    tall = domains * rows
    height, width = friction_ref.shape

    barrier = pltpu.get_barrier_semaphore()
    for off in range(1, groups):
        pl.semaphore_signal(barrier, inc=1, device_id=((g + off) % groups, d), device_id_type=MESH)
    for off in range(1, domains):
        pl.semaphore_signal(barrier, inc=1, device_id=(g, (d + off) % domains), device_id_type=MESH)
    pl.semaphore_wait(barrier, groups + domains - 2)

    def strip_rows(which):
        return pl.ds(pl.multiple_of(which * tall, tall), tall)

    def block_rows(which):
        return pl.ds(pl.multiple_of(which * rows, rows), rows)

    def send(src, dst, sems, off, device):
        copy = pltpu.make_async_remote_copy(
            src_ref=src, dst_ref=dst, send_sem=sems[0].at[off - 1], recv_sem=sems[1].at[off - 1],
            device_id=device, device_id_type=MESH,
        )
        copy.start()
        return copy

    copies = []
    for off in range(1, groups):
        other = (g + off) % groups
        copies.append(send(sums_ref.at[strip_rows(other)], strip_in.at[off - 1],
                           (send_a, recv_a), off, (other, d)))
    total = sums_ref[strip_rows(g), :]
    for copy in copies:
        copy.wait()
    for off in range(1, groups):
        total = total + strip_in[off - 1]
    strip[...] = total

    copies = []
    for off in range(1, domains):
        other = (d + off) % domains
        copies.append(send(strip.at[block_rows(other)], block_in.at[off - 1],
                           (send_b, recv_b), off, (g, other)))
    melted = strip[block_rows(d), :]
    for copy in copies:
        copy.wait()
    for off in range(1, domains):
        melted = melted + block_in[off - 1]
    ice = thick_ref[...] - THIN_RATE * melted
    ice_ref[...] = ice
    strips[g, block_rows(d), :] = ice

    copies = []
    for off in range(1, domains):
        other = (d + off) % domains
        copies.append(send(strips.at[g, block_rows(d)], strips.at[g, block_rows(d)],
                           (send_c, recv_c), off, (g, other)))
    for copy in copies:
        copy.wait()
    copies = []
    for off in range(1, groups):
        other = (g + off) % groups
        copies.append(send(strips.at[g], strips.at[g], (send_d, recv_d), off, (other, d)))
    for copy in copies:
        copy.wait()

    thickness = jnp.concatenate([strips[i] for i in range(groups)], axis=1)
    row = lax.broadcasted_iota(jnp.int32, (height, width), 0)
    col = lax.broadcasted_iota(jnp.int32, (height, width), 1)

    def west(value):
        return jnp.where(col == 0, 0.0, pltpu.roll(value, 1, 1))

    def east(value):
        return jnp.where(col == width - 1, 0.0, pltpu.roll(value, width - 1, 1))

    def south(value):
        return jnp.where(row == 0, 0.0, pltpu.roll(value, 1, 0))

    def north(value):
        return jnp.where(row == height - 1, 0.0, pltpu.roll(value, height - 1, 0))

    visc[...] = VISC_FLOOR + 0.5 * thickness * thickness
    diag[...] = friction_ref[...] + 2.0 * visc[...] + west(visc[...]) + south(visc[...])

    def operate(value):
        viscosity = visc[...]
        image = friction_ref[...] * value + viscosity * (2.0 * value - east(value) - north(value))
        image = image + west(viscosity) * (value - west(value))
        return image + south(viscosity) * (value - south(value))

    iterate[...] = velocity_ref[...]
    resid[...] = driving_ref[...] * thickness - operate(velocity_ref[...])
    direct[...] = resid[...] / diag[...]
    norm = jnp.sum(resid[...] * direct[...], keepdims=True)

    def sweep(_, norm):
        direction = direct[...]
        image = operate(direction)
        length = norm / jnp.sum(direction * image, keepdims=True)
        iterate[...] += length * direction
        residual = resid[...] - length * image
        resid[...] = residual
        precond = residual / diag[...]
        following = jnp.sum(residual * precond, keepdims=True)
        direct[...] = precond + following / norm * direction
        return following

    lax.fori_loop(0, ITERS - 1, sweep, norm)
    direction = direct[...]
    image = operate(direction)
    last = jnp.sum(resid[...] * (resid[...] / diag[...]), keepdims=True)
    length = last / jnp.sum(direction * image, keepdims=True)
    iterate[...] += length * direction
    out_ref[...] = iterate[block_rows(d), pl.ds(pl.multiple_of(g * cols, cols), cols)]


def local(tracers, mix_weights, neighbors, send_list, slot_cell, slot_owner, slot_node,
          thickness, friction, driving, velocity):
    levels, cells = tracers.shape[1:]
    groups = lax.axis_size("grp")
    domains = lax.axis_size("dom")
    devices = groups * domains
    slots = slot_cell.shape[0]
    rim = send_list.shape[0] // 2
    rows, cols = thickness.shape
    f32 = jnp.float32
    whole = pl.BlockSpec(memory_space=VMEM)
    scalars = pl.BlockSpec(memory_space=SMEM)
    anywhere = pl.BlockSpec(memory_space=pl.ANY)
    big = pltpu.CompilerParams(vmem_limit_bytes=BIG)

    shards = lax.all_gather(
        jnp.concatenate([thickness, friction, driving, velocity], axis=0), ("grp", "dom"), axis=0
    ).reshape(devices, 4, rows, cols)
    thick_table = shards[:, 0].reshape(devices * rows, cols)
    grids = [
        shards[:, i].reshape(groups, domains * rows, cols).transpose(1, 0, 2).reshape(
            domains * rows, groups * cols)
        for i in range(1, 4)
    ]

    halo = jax.ShapeDtypeStruct((2, levels, rim), f32)
    table, to_left, to_right = pl.pallas_call(
        turn_kernel,
        out_shape=(jax.ShapeDtypeStruct((2, cells, LANES), f32), halo, halo),
        in_specs=[scalars, whole],
        out_specs=(whole, whole, whole),
        scratch_shapes=[pltpu.VMEM((2, 2 * rim, LANES), f32)],
        compiler_params=big,
    )(send_list, tracers)
    forward = [(i, (i + 1) % domains) for i in range(domains)]
    backward = [(target, source) for source, target in forward]
    left = lax.ppermute(to_right, "dom", forward)
    right = lax.ppermute(to_left, "dom", backward)

    count = neighbors.shape[0]
    index = [neighbors[k] for k in range(count)]
    weight = [mix_weights[k] for k in range(count)]
    for place in range(LEAD):
        for k in range(count - 1, place, -1):
            swap = index[k] < index[k - 1]
            index[k - 1], index[k] = (
                jnp.where(swap, index[k], index[k - 1]), jnp.where(swap, index[k - 1], index[k]))
            weight[k - 1], weight[k] = (
                jnp.where(swap, weight[k], weight[k - 1]), jnp.where(swap, weight[k - 1], weight[k]))
    lead_index, lead_weight = jnp.stack(index[:LEAD]), jnp.stack(weight[:LEAD])
    rest_index, rest_weight = jnp.stack(index[LEAD:]), jnp.stack(weight[LEAD:])
    inside = lead_index < cells
    near_index = jnp.where(inside, lead_index, 0)
    near_weight = jnp.where(inside, lead_weight, 0.0)
    far_weight = jnp.where(inside, 0.0, lead_weight)
    flags = jnp.any(jnp.logical_not(inside).reshape(LEAD, cells // GROUP, GROUP), axis=(0, 2)).astype(jnp.int32)

    own_weight = (1.0 - 2.0 * VERT_MIX) - jnp.sum(mix_weights, axis=0, keepdims=True)
    block = 1024

    def listed(number):
        return pl.BlockSpec((number, block), lambda i: (0, i), memory_space=SMEM)

    columns = pl.BlockSpec((2, block, LANES), lambda i: (0, i, 0))
    near = pl.pallas_call(
        near_kernel,
        grid=(cells // block,),
        out_shape=jax.ShapeDtypeStruct((2, cells, LANES), f32),
        in_specs=[
            listed(LEAD), listed(LEAD),
            pl.BlockSpec((1, block), lambda i: (0, i)),
            pl.BlockSpec((2, levels, block), lambda i: (0, 0, i)),
            anywhere,
        ],
        out_specs=columns,
        scratch_shapes=[pltpu.VMEM((2, cells, LANES), f32), pltpu.SemaphoreType.DMA],
        compiler_params=big,
        cost_estimate=pl.CostEstimate(flops=100_000_000, bytes_accessed=130_000_000, transcendentals=0),
    )(near_index, near_weight, own_weight, tracers, table)
    edge = pl.BlockSpec((2, levels, rim), lambda i: (0, 0, 0))
    mixed = pl.pallas_call(
        far_kernel,
        grid=(cells // block,),
        out_shape=jax.ShapeDtypeStruct((2, cells, LANES), f32),
        in_specs=[
            scalars, listed(count - LEAD), listed(count - LEAD), listed(LEAD), listed(LEAD),
            anywhere, edge, edge, columns,
        ],
        out_specs=columns,
        scratch_shapes=[pltpu.VMEM((2, cells + 2 * rim, LANES), f32), pltpu.SemaphoreType.DMA],
        compiler_params=big,
        cost_estimate=pl.CostEstimate(flops=200_000_000, bytes_accessed=200_000_000, transcendentals=0),
    )(flags, rest_index, rest_weight, lead_index, far_weight, table, left, right, near)

    grid_row = slot_owner[:, 0] * rows + slot_node // cols
    grid_col = slot_node % cols
    ocean, sums = pl.pallas_call(
        melt_kernel,
        out_shape=(jax.ShapeDtypeStruct((2, levels, cells), f32),
                   jax.ShapeDtypeStruct((devices * rows, cols), f32)),
        in_specs=[scalars, whole, whole, whole, whole, anywhere],
        out_specs=(whole, whole),
        scratch_shapes=[
            pltpu.VMEM((2, cells, LANES), f32),
            pltpu.VMEM((slots, LANES), f32),
            pltpu.VMEM((slots, LANES), f32),
            pltpu.VMEM((slots, LANES), f32),
            pltpu.SemaphoreType.DMA,
        ],
        compiler_params=big,
    )(slot_cell, grid_row[:, None], grid_row[None, :], grid_col[:, None], thick_table, mixed)

    grid_shape = (domains * rows, groups * cols)
    dma = pltpu.SemaphoreType.DMA
    ice, iterate = pl.pallas_call(
        functools.partial(ice_kernel, groups, domains),
        out_shape=(jax.ShapeDtypeStruct((rows, cols), f32),) * 2,
        in_specs=[whole] * 5,
        out_specs=(whole, whole),
        scratch_shapes=[
            pltpu.VMEM((groups - 1, domains * rows, cols), f32),
            pltpu.VMEM((domains * rows, cols), f32),
            pltpu.VMEM((domains - 1, rows, cols), f32),
            pltpu.VMEM((groups, domains * rows, cols), f32),
        ] + [pltpu.VMEM(grid_shape, f32)] * 5 + [
            dma((groups - 1,)), dma((groups - 1,)), dma((domains - 1,)), dma((domains - 1,)),
            dma((domains - 1,)), dma((domains - 1,)), dma((groups - 1,)), dma((groups - 1,)),
        ],
        compiler_params=pltpu.CompilerParams(
            collective_id=0, has_side_effects=True, vmem_limit_bytes=BIG
        ),
    )(sums, thickness, *grids)
    return ocean, ice, iterate


def solution(mesh):
    return jax.shard_map(
        local,
        mesh=mesh,
        in_specs=(
            P(None, None, ("grp", "dom")),
            P(None, ("grp", "dom")),
            P(None, ("grp", "dom")),
            P(("grp", "dom")),
            P(("grp", "dom")),
            P(("grp", "dom"), None),
            P(("grp", "dom")),
            P("dom", "grp"),
            P("dom", "grp"),
            P("dom", "grp"),
            P("dom", "grp"),
        ),
        out_specs=(P(None, None, ("grp", "dom")), P("dom", "grp"), P("dom", "grp")),
        check_vma=False,
    )
```
